256 devices in a mesh: seq: 32 (over y, x, core), head: 8 (over z).
Axes of the slice: x: 4, y: 4, z: 8, core: 2. Of those that a mesh axis runs over, the one named last changes fastest.
Arguments:
- queries: bfloat16 [8192, 4096], P('seq', 'head'), may hold values from -0.59765625 to 0.59765625
- keys: bfloat16 [8192, 4096], P('seq', 'head'), may hold values from -0.59765625 to 0.59765625
- values: bfloat16 [8192, 4096], P('seq', 'head'), may hold values from -6 to 6
- log_decay: float32 [32, 8192], P('head', 'seq'), may hold values from -0.8 to 0, as said below
- lengths: int32 [16], replicated, may hold values from 1 to 2048, as said below
- out_weight: bfloat16 [4096, 4096], P('seq', 'head'), may hold values from -0.09375 to 0.09375
- out_grad: bfloat16 [8192, 4096], P('seq', 'head'), may hold values from -0.29882812 to 0.29882812
Outputs:
- mixed: bfloat16 [8192, 4096], P('seq', 'head')
- grad_queries: bfloat16 [8192, 4096], P('seq', 'head')
- grad_keys: bfloat16 [8192, 4096], P('seq', 'head')
- grad_values: bfloat16 [8192, 4096], P('seq', 'head')
- grad_weight: float32 [4096, 4096], P('seq', 'head')
The draws below stay inside these ranges and needn't reach their ends.
Inputs may be any that keep to these rules, and one draw needn't show every extreme that they name: `log_decay`: every entry is negative; tokens where a document starts cut the state whatever their value. The 16 lengths sum to 8192; the longest document has exactly 2048 tokens.
All inputs are finite; a program needn't handle non-finite values.
Results may differ from the reference program's by a relative error of at most 0.015.
Values may be sent and summed in bfloat16 or wider, within the bound.
No kernel may reach another device: no remote copies, remote signals or barrier semaphores. Data moves between devices by JAX's collectives and lax.ppermute only.
A program may use at most 64 MiB of HBM per device.

```python
import math
import jax
import jax.numpy as jnp
from jax import lax

D = 4096
ATTENTION_HEADS = 32
HD = 128
TOK_DEV = 256
NDOCS = 16
PACKED_TOKENS = 8192
MOST = 2048


def draw_log_decay(key, part):
    random_split_keys = jax.random.split(key, 7)
    fast_top = 1.0 / 40.0
    base_low = 0.05 / MOST
    baseline_decay_rate = jnp.exp(jax.random.uniform(random_split_keys[0], (ATTENTION_HEADS, 1), minval=math.log(base_low), maxval=math.log(fast_top)))
    shards = PACKED_TOKENS // TOK_DEV
    damping_factor = jnp.exp(jax.random.uniform(random_split_keys[3], (ATTENTION_HEADS, shards, 1), minval=-0.5, maxval=0.5))
    damping_factor = jnp.broadcast_to(damping_factor, (ATTENTION_HEADS, shards, TOK_DEV)).reshape(ATTENTION_HEADS, PACKED_TOKENS)
    random_jitter = jnp.exp(jax.random.uniform(random_split_keys[4], (ATTENTION_HEADS, PACKED_TOKENS), minval=-0.4, maxval=0.4))
    spike_position = jax.random.uniform(random_split_keys[5], (ATTENTION_HEADS, PACKED_TOKENS)) < 4.0 / PACKED_TOKENS
    spike_loss_value = jnp.log(jax.random.uniform(random_split_keys[6], (ATTENTION_HEADS, PACKED_TOKENS), minval=0.5, maxval=0.8))
    return (-(baseline_decay_rate * damping_factor * random_jitter) + jnp.where(spike_position, spike_loss_value, 0.0)).astype(jnp.float32)


def draw_lengths(key, part):
    others = NDOCS - 3
    lowest = max(TOK_DEV // 4, 1)
    highest = 3 * TOK_DEV // 4 + 1
    offsets = jax.random.randint(jax.random.fold_in(key, 12), (2,), lowest, highest, dtype=jnp.int32)
    first_long = (MOST - offsets[0]).astype(jnp.int32)
    third_long = (MOST - offsets[1]).astype(jnp.int32)
    spare = (MOST + offsets[0] + offsets[1] - others).astype(jnp.int32)
    weights = jax.random.randint(jax.random.fold_in(key, 11), (others,), 50, 101, dtype=jnp.int32)
    running = jnp.cumsum(weights, dtype=jnp.int32)
    total_weight = running[-1]
    bounds = spare * running // total_weight
    earlier = jnp.concatenate([jnp.zeros((1,), jnp.int32), bounds[:-1]])
    rest = (1 + bounds - earlier).astype(jnp.int32)
    longs = jnp.stack([first_long, jnp.asarray(MOST, jnp.int32), third_long]).astype(jnp.int32)
    return jnp.concatenate([longs, rest]).astype(jnp.int32)


def spiked(values, rng, source, target, parts, factor):
    owner, partner = [(jnp.arange(values.shape[axis_at]) // (values.shape[axis_at] // parts)).reshape([-1 if axis == axis_at else 1 for axis in range(values.ndim)]) for axis_at in (source, target)]
    chosen = jax.random.permutation(rng, parts)[partner]
    strong = (owner == chosen) | (owner == (partner + parts // 2) % parts)
    return jnp.where(strong, factor * values, values)


def steps_of(rng, dims, pieces, low, high):
    level = 1.0
    for dim, shards_of in pieces:
        steps = jax.random.uniform(jax.random.fold_in(jax.random.fold_in(rng, 6), dim), (shards_of,), jnp.float32, low / len(pieces), high / len(pieces))
        level = level * jnp.repeat(jnp.exp(steps), dims[dim] // shards_of).reshape((-1,) + (1,) * (len(dims) - 1 - dim))
    return level


def noise(own_key, dims, width, reach, cuts=(), kind=jnp.bfloat16):
    factor_of = steps_of(own_key, dims, cuts, -0.22, 0.18) if cuts else 1.0
    values = jax.random.normal(own_key, dims, jnp.float32) * width * factor_of
    return jnp.minimum(jnp.maximum(values, -reach), reach).astype(kind)


def gaussian_with(rng, extent, scale, limit, cuts, heavy, kind=jnp.bfloat16):
    drawn = scale * jax.random.normal(rng, extent, jnp.float32)
    if cuts:
        drawn = drawn * steps_of(rng, extent, cuts, -0.22, 0.18)
    return jnp.clip(spiked(drawn, jax.random.fold_in(rng, 3), *heavy), -limit, limit).astype(kind)


def setup_inputs(seed: int = 0) -> dict:
    seeds = jax.random.split(jax.random.key(seed), 8)
    return {
        "queries": noise(seeds[0], (PACKED_TOKENS, ATTENTION_HEADS * HD), 0.1, 0.59765625, ((0, 32), (1, 8))),
        "keys": noise(seeds[1], (PACKED_TOKENS, ATTENTION_HEADS * HD), 0.1, 0.59765625, ((0, 32), (1, 8))),
        "values": noise(seeds[2], (PACKED_TOKENS, ATTENTION_HEADS * HD), 1.0, 6.0, ((0, 32), (1, 8))),
        "log_decay": draw_log_decay(jax.random.fold_in(seeds[7], 71), 0),
        "lengths": draw_lengths(jax.random.fold_in(seeds[7], 71), 0),
        "out_weight": noise(seeds[5], (D, ATTENTION_HEADS * HD), (ATTENTION_HEADS * HD) ** -0.5, 0.09375, ((0, 32), (1, 8))),
        "out_grad": gaussian_with(seeds[6], (PACKED_TOKENS, D), 0.05, 0.29882812, ((0, 32), (1, 8)), (0, 1, 32, 2.75)),
    }


HIGH = lax.Precision.HIGHEST


def doc_index(lengths, positions):
    starts = jnp.cumsum(lengths, dtype=jnp.int32) - lengths
    above = (positions[:, None] >= starts[None, :]).astype(jnp.int32)
    return jnp.sum(above, axis=1, dtype=jnp.int32) - 1


def block_masks(log_decay, docs, prev_doc, last_doc, next_doc):
    count = docs.shape[0]
    cumul = jnp.cumsum(log_decay, axis=1)
    order = jnp.arange(count, dtype=jnp.int32)
    joint = jnp.logical_and(order[:, None] >= order[None, :], docs[:, None] == docs[None, :])[None]
    spread = jnp.where(joint, cumul[:, :, None] - cumul[:, None, :], 0.0)
    decay = jnp.where(joint, jnp.exp(spread), 0.0)
    zero = jnp.zeros_like(cumul)
    tail = cumul[:, -1:] - cumul
    enter = jnp.where((docs == prev_doc)[None], jnp.exp(cumul), zero)
    keep = jnp.where((docs == last_doc)[None], jnp.exp(tail), zero)
    leave = jnp.where((docs == next_doc)[None], jnp.exp(tail), zero)
    through = jnp.where(prev_doc == last_doc, jnp.exp(cumul[:, -1]), jnp.zeros_like(cumul[:, -1]))
    return decay, enter, keep, leave, through


def reference(queries, keys, values, log_decay, lengths, out_weight, out_grad):
    blocks = PACKED_TOKENS // TOK_DEV
    rows = TOK_DEV

    def split(x):
        return x.reshape(blocks, rows, ATTENTION_HEADS, HD)

    qs, ks, vs = split(queries), split(keys), split(values)
    decays = log_decay.reshape(ATTENTION_HEADS, blocks, rows).transpose(1, 0, 2)
    docs = doc_index(lengths, jnp.arange(PACKED_TOKENS, dtype=jnp.int32)).reshape(blocks, rows)
    starts = jnp.arange(blocks, dtype=jnp.int32) * rows
    prevs = doc_index(lengths, (starts - 1).astype(jnp.int32))
    lasts = doc_index(lengths, (starts + rows - 1).astype(jnp.int32))
    nexts = doc_index(lengths, (starts + rows).astype(jnp.int32))

    def forward(state, item):
        qb, kb, vb, lb, db, pb, tb, nb = item
        decay, enter, keep, leave, through = block_masks(lb, db, pb, tb, nb)
        q32, k32, v32 = qb.astype(jnp.float32), kb.astype(jnp.float32), vb.astype(jnp.float32)
        scores = jnp.einsum('the,she->hts', q32, k32)
        attn = lax.optimization_barrier((scores * decay).astype(jnp.bfloat16)).astype(jnp.float32)
        local = jnp.einsum('hts,shf->thf', attn, v32)
        carry = jnp.einsum('the,hef->thf', q32, state, precision=HIGH) * enter.T[:, :, None]
        out = (local + carry).astype(jnp.bfloat16)
        summary = jnp.einsum('the,thf->hef', k32 * keep.T[:, :, None], v32, precision=HIGH)
        return through[:, None, None] * state + summary, (out, state)

    init = jnp.zeros((ATTENTION_HEADS, HD, HD), jnp.float32)
    items = (qs, ks, vs, decays, docs, prevs, lasts, nexts)
    _, (outs, states) = lax.scan(forward, init, items)
    attended = outs.reshape(PACKED_TOKENS, ATTENTION_HEADS * HD)
    mixed = jnp.dot(attended, out_weight.T, preferred_element_type=jnp.float32).astype(jnp.bfloat16)
    grad_att = jnp.dot(out_grad, out_weight, preferred_element_type=jnp.float32).astype(jnp.bfloat16)
    grad_weight = jnp.dot(out_grad.T, attended, preferred_element_type=jnp.float32)
    gs = split(grad_att)

    def backward(carry, item):
        qb, kb, vb, gb, lb, db, pb, tb, nb, state = item
        decay, enter, keep, leave, through = block_masks(lb, db, pb, tb, nb)
        q32, k32, v32, g32 = qb.astype(jnp.float32), kb.astype(jnp.float32), vb.astype(jnp.float32), gb.astype(jnp.float32)
        scores = jnp.einsum('the,she->hts', q32, k32)
        attn = lax.optimization_barrier((scores * decay).astype(jnp.bfloat16)).astype(jnp.float32)
        pulls = jnp.einsum('thf,shf->hts', g32, v32)
        back = lax.optimization_barrier((pulls * decay).astype(jnp.bfloat16)).astype(jnp.float32)
        dq = jnp.einsum('hts,she->the', back, k32) + jnp.einsum('hef,thf->the', state, g32, precision=HIGH) * enter.T[:, :, None]
        dk = jnp.einsum('hts,the->she', back, q32) + jnp.einsum('hef,thf->the', carry, v32, precision=HIGH) * leave.T[:, :, None]
        dv = jnp.einsum('hts,thf->shf', attn, g32) + jnp.einsum('hef,the->thf', carry, k32, precision=HIGH) * leave.T[:, :, None]
        summary = jnp.einsum('the,thf->hef', q32 * enter.T[:, :, None], g32, precision=HIGH)
        new_carry = through[:, None, None] * carry + summary
        return new_carry, (dq.astype(jnp.bfloat16), dk.astype(jnp.bfloat16), dv.astype(jnp.bfloat16))

    items_back = (qs, ks, vs, gs, decays, docs, prevs, lasts, nexts, states)
    _, (dqs, dks, dvs) = lax.scan(backward, init, items_back, reverse=True)
    shape = (PACKED_TOKENS, ATTENTION_HEADS * HD)
    return mixed, dqs.reshape(shape), dks.reshape(shape), dvs.reshape(shape), grad_weight
```

```python
import functools

import jax
import jax.numpy as jnp
from jax import lax
from jax.experimental import pallas as pl
from jax.experimental.pallas import tpu as pltpu
from jax.sharding import Mesh, PartitionSpec as P

F32 = jnp.float32
BF16 = jnp.bfloat16
HIGH = lax.Precision.HIGHEST
SIDE = 4
LONG = 8
HEADS = 4
HD = 128
ROWS = 256
HALF = 256
STATE = HEADS * HD
PAY = STATE + 16
DOCS = 16
VMEM = pl.BlockSpec(memory_space=pltpu.VMEM)
SMEM = pl.BlockSpec(memory_space=pltpu.SMEM)


def call(kernel, outs, specs, flops):
    return pl.pallas_call(
        kernel,
        out_shape=[jax.ShapeDtypeStruct(s, d) for s, d in outs],
        in_specs=specs,
        out_specs=[VMEM] * len(outs),
        compiler_params=pltpu.CompilerParams(vmem_limit_bytes=48 * 2**20),
        cost_estimate=pl.CostEstimate(flops=flops, bytes_accessed=2**20, transcendentals=0),
    )


def dot(a, b, dims, precision=None):
    return lax.dot_general(a, b, (dims, ((), ())), precision=precision, preferred_element_type=F32)


NN = ((1,), (0,))
NT = ((1,), (1,))
TN = ((0,), (0,))


class Masks:
    def __init__(self, len_ref, at_ref, ld_ref):
        first = at_ref[0]
        pos_r = first + lax.broadcasted_iota(jnp.int32, (1, ROWS), 1)
        pos_c = first + lax.broadcasted_iota(jnp.int32, (ROWS, 1), 0)
        doc_r = jnp.full((1, ROWS), -1, jnp.int32)
        doc_c = jnp.full((ROWS, 1), -1, jnp.int32)
        edge = [jnp.int32(-1)] * 3
        start = jnp.int32(0)
        for j in range(DOCS):
            doc_r = doc_r + jnp.where(pos_r >= start, 1, 0)
            doc_c = doc_c + jnp.where(pos_c >= start, 1, 0)
            for n, p in enumerate((first - 1, first + ROWS - 1, first + ROWS)):
                edge[n] = edge[n] + jnp.where(p >= start, 1, 0)
            start = start + len_ref[j]
        prev, last, after = edge
        row = lax.broadcasted_iota(jnp.int32, (ROWS, ROWS), 0)
        col = lax.broadcasted_iota(jnp.int32, (ROWS, ROWS), 1)
        ld = ld_ref[...]
        self.cum_r = dot(ld, jnp.where(row <= col, 1.0, 0.0).astype(F32), NN, HIGH)
        self.cum_c = dot(jnp.where(col <= row, 1.0, 0.0).astype(F32), ld, NT, HIGH)
        self.joint = jnp.logical_and(row >= col, doc_c == doc_r)
        self.first_doc, self.last_doc, self.next_doc = doc_c == prev, doc_c == last, doc_c == after
        self.whole = prev == last

    def decay(self, h):
        gap = self.cum_c[:, h : h + 1] - self.cum_r[h : h + 1, :]
        return jnp.where(self.joint, jnp.exp(jnp.where(self.joint, gap, 0.0)), 0.0)

    def total(self, h):
        return self.cum_r[h : h + 1, ROWS - 1 : ROWS]

    def enter(self, h):
        return jnp.where(self.first_doc, jnp.exp(self.cum_c[:, h : h + 1]), 0.0)

    def tail(self, h):
        return jnp.exp(self.total(h) - self.cum_c[:, h : h + 1])

    def keep(self, h):
        return jnp.where(self.last_doc, self.tail(h), 0.0)

    def leave(self, h):
        return jnp.where(self.next_doc, self.tail(h), 0.0)

    def through(self, h):
        return jnp.where(self.whole, jnp.exp(self.total(h)), 0.0)


def head(h):
    return slice(h * HD, (h + 1) * HD)


def put_factors(ref, factors):
    row = lax.broadcasted_iota(jnp.int32, (16, HD), 0)
    block = jnp.zeros((16, HD), F32)
    for h, f in enumerate(factors):
        high = f.astype(BF16).astype(F32)
        block = block + jnp.where(row == h, high, 0.0) + jnp.where(row == HEADS + h, f - high, 0.0)
    ref[STATE:PAY, :] = block.astype(BF16)


def take(ref):
    tail = ref[STATE:PAY, :].astype(F32)
    states = [ref[head(h), :].astype(F32) for h in range(HEADS)]
    factors = [tail[h : h + 1, 0:1] + tail[HEADS + h : HEADS + h + 1, 0:1] for h in range(HEADS)]
    return states, factors


def chain(a_ref, b_ref, c_ref):
    (sa, fa), (sb, fb), (sc, fc) = take(a_ref), take(b_ref), take(c_ref)
    states = [sa[h] + fa[h] * (sb[h] + fb[h] * sc[h]) for h in range(HEADS)]
    return states, [fa[h] * fb[h] * fc[h] for h in range(HEADS)]


def first_kernel(len_ref, at_ref, ld_ref, q_ref, k_ref, v_ref, pay_ref, local_ref):
    m = Masks(len_ref, at_ref, ld_ref)
    for h in range(HEADS):
        k, v = k_ref[:, head(h)], v_ref[:, head(h)]
        kept = (k.astype(F32) * m.keep(h)).astype(BF16)
        pay_ref[head(h), :] = dot(kept, v, TN).astype(BF16)
        attn = (dot(q_ref[:, head(h)], k, NT) * m.decay(h)).astype(BF16)
        local_ref[:, head(h)] = dot(attn, v, NN)
    put_factors(pay_ref, [m.through(h) for h in range(HEADS)])


def window_kernel(a_ref, b_ref, c_ref, pay_ref):
    states, factors = chain(a_ref, b_ref, c_ref)
    for h in range(HEADS):
        pay_ref[head(h), :] = states[h].astype(BF16)
    put_factors(pay_ref, factors)


def attend_kernel(len_ref, at_ref, ld_ref, q_ref, local_ref, a_ref, b_ref, c_ref, att_ref, state_ref):
    m = Masks(len_ref, at_ref, ld_ref)
    states, _ = chain(a_ref, b_ref, c_ref)
    for h in range(HEADS):
        state = states[h].astype(BF16)
        state_ref[head(h), :] = state
        carried = dot(q_ref[:, head(h)], state, NN) * m.enter(h)
        att_ref[:, head(h)] = (local_ref[:, head(h)] + carried).astype(BF16)


def back_kernel(len_ref, at_ref, ld_ref, q_ref, own_ref, other_ref, pay_ref, g_ref):
    m = Masks(len_ref, at_ref, ld_ref)
    for h in range(HEADS):
        g = (own_ref[:, head(h)] + other_ref[:, head(h)].astype(F32)).astype(BF16)
        g_ref[:, head(h)] = g
        entered = (q_ref[:, head(h)].astype(F32) * m.enter(h)).astype(BF16)
        pay_ref[head(h), :] = dot(entered, g, TN).astype(BF16)
    put_factors(pay_ref, [m.through(h) for h in range(HEADS)])


def grads_kernel(
    len_ref, at_ref, ld_ref, q_ref, k_ref, v_ref, g_ref, state_ref, a_ref, b_ref, c_ref, dq_ref, dk_ref, dv_ref
):
    m = Masks(len_ref, at_ref, ld_ref)
    carries, _ = chain(a_ref, b_ref, c_ref)
    for h in range(HEADS):
        q, k, v, g = (r[:, head(h)] for r in (q_ref, k_ref, v_ref, g_ref))
        decay, leave, carry = m.decay(h), m.leave(h), carries[h].astype(BF16)
        attn = (dot(q, k, NT) * decay).astype(BF16)
        back = (dot(g, v, NT) * decay).astype(BF16)
        dq = dot(back, k, NN) + dot(g, state_ref[head(h), :], NT) * m.enter(h)
        dk = dot(back, q, TN) + dot(v, carry, NT) * leave
        dv = dot(attn, g, TN) + dot(k, carry, NN) * leave
        dq_ref[:, head(h)] = dq.astype(BF16)
        dk_ref[:, head(h)] = dk.astype(BF16)
        dv_ref[:, head(h)] = dv.astype(BF16)


def chip_of(j, y, x, sign):
    far, near = j // 2, 2 * (j % 2)
    dy = lax.rem(sign * (far - y) + SIDE, SIDE)
    return dy, [lax.rem(sign * (near + e - x) + SIDE, SIDE) for e in range(2)]


def weight_part(wa_ref, wb_ref, j, at_ref):
    ry, rx = chip_of(j, at_ref[1], at_ref[2], -1)
    left = jnp.concatenate([wa_ref[ry, r] for r in rx], axis=0)
    right = jnp.concatenate([wb_ref[r, ry] for r in rx], axis=0)
    return jnp.concatenate([left, right], axis=1)


def pull_kernel(at_ref, g_ref, wa_ref, wb_ref, own_ref, send_ref):
    total = jnp.zeros((2 * ROWS, STATE), F32)
    for j in range(LONG):
        slot = lax.rem(at_ref[3] - j + LONG, LONG)
        total = total + dot(g_ref[slot], weight_part(wa_ref, wb_ref, j, at_ref), NN)
    own_ref[...] = total[:ROWS]
    send_ref[...] = total[ROWS:].astype(BF16)


def mix_kernel(at_ref, own_ref, other_ref, wa_ref, wb_ref, out_ref):
    for j in range(LONG):
        w = weight_part(wa_ref, wb_ref, j, at_ref)
        out_ref[j, :ROWS] = dot(own_ref[...], w, NT).astype(BF16)
        out_ref[j, ROWS:] = dot(other_ref[...], w, NT).astype(BF16)


def weight_grad_kernel(at_ref, g_ref, own_ref, other_ref, ra_ref, rb_ref):
    for j in range(LONG):
        slot = lax.rem(at_ref[3] - j + LONG, LONG)
        dy, dx = chip_of(j, at_ref[1], at_ref[2], 1)
        part = dot(g_ref[slot, :ROWS], own_ref[...], TN) + dot(g_ref[slot, ROWS:], other_ref[...], TN)
        part = part.astype(BF16)
        for e in range(2):
            rows = slice(e * HD, (e + 1) * HD)
            ra_ref[dy, dx[e]] = part[rows, :HALF]
            rb_ref[dx[e], dy] = part[rows, HALF:]


def ring(value, axis, steps):
    count = lax.axis_size(axis)
    return lax.ppermute(value, axis, [(i, (i + steps) % count) for i in range(count)])


def line(value, steps):
    count = SIDE * SIDE * 2
    pairs = [(i, i + steps) for i in range(count) if 0 <= i + steps < count]
    return lax.ppermute(value, ("y", "x", "core"), pairs)


def gather_side(value, axis):
    return jnp.stack([value] + [ring(value, axis, s) for s in (1, 2, -1)])


def scatter_side(value, axis):
    parts = [value[0]] + [ring(value[s], axis, s if s < 3 else -1) for s in (1, 2, 3)]
    return functools.reduce(jnp.add, [p.astype(F32) for p in parts])


def gather_long(value):
    found = {0: value}
    right = left = value
    for s in range(1, LONG // 2 + 1):
        right = ring(right, "z", 1)
        found[s] = right
        if s < LONG // 2:
            left = ring(left, "z", -1)
            found[LONG - s] = left
    return jnp.stack([found[s] for s in range(LONG)])


def swap(value):
    return ring(value, "core", 1)


def parity(value):
    return [jnp.concatenate([value[:, (2 * e + c) * HD : (2 * e + c + 1) * HD] for e in range(2)], 1) for c in range(2)]


def body(q, k, v, log_decay, lengths, weight, out_grad):
    y, x, c, z = (lax.axis_index(a) for a in ("y", "x", "core", "z"))
    at = jnp.stack([((y * SIDE + x) * 2 + c) * ROWS, y, x, z]).astype(jnp.int32)
    lead = (lengths, at, log_decay)
    lead_specs = [SMEM, SMEM, VMEM]
    even, odd = parity(out_grad)
    mine, yours = jnp.where(c == 0, even, odd), jnp.where(c == 0, odd, even)
    grads = gather_long(jnp.concatenate([mine, swap(yours)], axis=0))
    wa = gather_side(gather_side(weight[:, :HALF], "x"), "y")
    wb = gather_side(gather_side(weight[:, HALF:], "y"), "x")
    wide = ((ROWS, STATE), BF16)
    pay, local = call(
        first_kernel, [((PAY, HD), BF16), ((ROWS, STATE), F32)], lead_specs + [VMEM] * 3, 2**28
    )(*lead, q, k, v)
    window = call(window_kernel, [((PAY, HD), BF16)], [VMEM] * 3, 2**20)
    [pay] = window(pay, line(pay, 1), line(pay, 2))
    att, state = call(attend_kernel, [wide, ((STATE, HD), BF16)], lead_specs + [VMEM] * 5, 2**26)(
        *lead, q, local, line(pay, 1), line(pay, 4), line(pay, 7)
    )
    att_other = swap(att)
    [mixed] = call(mix_kernel, [((LONG, 2 * ROWS, HALF), BF16)], [SMEM] + [VMEM] * 4, 2**30)(
        at, att, att_other, wa, wb
    )
    mixed = lax.psum_scatter(mixed, "z", scatter_dimension=0)
    mixed_other = swap(mixed[ROWS:])
    mixed = mixed[:ROWS]
    even, odd = jnp.where(c == 0, mixed, mixed_other), jnp.where(c == 0, mixed_other, mixed)
    mixed = jnp.concatenate([even[:, :HD], odd[:, :HD], even[:, HD:], odd[:, HD:]], axis=1)
    own, send = call(pull_kernel, [((ROWS, STATE), F32), wide], [SMEM] + [VMEM] * 3, 2**30)(at, grads, wa, wb)
    back, g = call(back_kernel, [((PAY, HD), BF16), wide], lead_specs + [VMEM] * 3, 2**26)(
        *lead, q, own, swap(send)
    )
    [back] = window(back, line(back, -1), line(back, -2))
    grid = ((SIDE, SIDE, HD, HALF), BF16)
    ra, rb = call(weight_grad_kernel, [grid, grid], [SMEM] + [VMEM] * 3, 2**30)(at, grads, att, att_other)
    ra = scatter_side(scatter_side(ra, "y").astype(BF16), "x")
    rb = scatter_side(scatter_side(rb, "x").astype(BF16), "y")
    dq, dk, dv = call(grads_kernel, [wide] * 3, lead_specs + [VMEM] * 8, 2**29)(
        *lead, q, k, v, g, state, line(back, -1), line(back, -4), line(back, -7)
    )
    return mixed, dq, dk, dv, jnp.concatenate([ra, rb], axis=1)


def solution(mesh):
    fine = Mesh(mesh.devices.reshape(SIDE, SIDE, 2, LONG), ("y", "x", "core", "z"))
    seq = ("y", "x", "core")
    wide = P(seq, "z")
    return jax.shard_map(
        body,
        mesh=fine,
        in_specs=(wide, wide, wide, P("z", seq), P(), wide, wide),
        out_specs=(wide,) * 5,
        check_vma=False,
    )
```

```python
import functools

import jax
import jax.numpy as jnp
from jax import lax
from jax.experimental import pallas as pl
from jax.experimental.pallas import tpu as pltpu
from jax.sharding import Mesh, PartitionSpec as P

F32 = jnp.float32
BF16 = jnp.bfloat16
HIGH = lax.Precision.HIGHEST
SIDE = 4
LONG = 8
HEADS = 4
HD = 128
ROWS = 256
HALF = 256
STATE = HEADS * HD
PAY = STATE + 16
DOCS = 16
VMEM = pl.BlockSpec(memory_space=pltpu.VMEM)
SMEM = pl.BlockSpec(memory_space=pltpu.SMEM)


def call(kernel, outs, specs, flops):
    return pl.pallas_call(
        kernel,
        out_shape=[jax.ShapeDtypeStruct(s, d) for s, d in outs],
        in_specs=specs,
        out_specs=[VMEM] * len(outs),
        compiler_params=pltpu.CompilerParams(vmem_limit_bytes=48 * 2**20),
        cost_estimate=pl.CostEstimate(flops=flops, bytes_accessed=2**20, transcendentals=0),
    )


def dot(a, b, dims, precision=None):
    return lax.dot_general(a, b, (dims, ((), ())), precision=precision, preferred_element_type=F32)


NN = ((1,), (0,))
NT = ((1,), (1,))
TN = ((0,), (0,))


class Masks:
    def __init__(self, len_ref, at_ref, ld_ref):
        first = at_ref[0]
        pos_r = first + lax.broadcasted_iota(jnp.int32, (1, ROWS), 1)
        pos_c = first + lax.broadcasted_iota(jnp.int32, (ROWS, 1), 0)
        doc_r = jnp.full((1, ROWS), -1, jnp.int32)
        doc_c = jnp.full((ROWS, 1), -1, jnp.int32)
        edge = [jnp.int32(-1)] * 3
        start = jnp.int32(0)
        for j in range(DOCS):
            doc_r = doc_r + jnp.where(pos_r >= start, 1, 0)
            doc_c = doc_c + jnp.where(pos_c >= start, 1, 0)
            for n, p in enumerate((first - 1, first + ROWS - 1, first + ROWS)):
                edge[n] = edge[n] + jnp.where(p >= start, 1, 0)
            start = start + len_ref[j]
        prev, last, after = edge
        row = lax.broadcasted_iota(jnp.int32, (ROWS, ROWS), 0)
        col = lax.broadcasted_iota(jnp.int32, (ROWS, ROWS), 1)
        ld = ld_ref[...]
        self.cum_r = dot(ld, jnp.where(row <= col, 1.0, 0.0).astype(F32), NN, HIGH)
        self.cum_c = dot(jnp.where(col <= row, 1.0, 0.0).astype(F32), ld, NT, HIGH)
        self.joint = jnp.logical_and(row >= col, doc_c == doc_r)
        self.first_doc, self.last_doc, self.next_doc = doc_c == prev, doc_c == last, doc_c == after
        self.whole = prev == last

    def decay(self, h):
        gap = self.cum_c[:, h : h + 1] - self.cum_r[h : h + 1, :]
        return jnp.where(self.joint, jnp.exp(jnp.where(self.joint, gap, 0.0)), 0.0)

    def total(self, h):
        return self.cum_r[h : h + 1, ROWS - 1 : ROWS]

    def enter(self, h):
        return jnp.where(self.first_doc, jnp.exp(self.cum_c[:, h : h + 1]), 0.0)

    def tail(self, h):
        return jnp.exp(self.total(h) - self.cum_c[:, h : h + 1])

    def keep(self, h):
        return jnp.where(self.last_doc, self.tail(h), 0.0)

    def leave(self, h):
        return jnp.where(self.next_doc, self.tail(h), 0.0)

    def through(self, h):
        return jnp.where(self.whole, jnp.exp(self.total(h)), 0.0)


def head(h):
    return slice(h * HD, (h + 1) * HD)


def put_factors(ref, factors):
    row = lax.broadcasted_iota(jnp.int32, (16, HD), 0)
    block = jnp.zeros((16, HD), F32)
    for h, f in enumerate(factors):
        high = f.astype(BF16).astype(F32)
        block = block + jnp.where(row == h, high, 0.0) + jnp.where(row == HEADS + h, f - high, 0.0)
    ref[STATE:PAY, :] = block.astype(BF16)


def take(ref):
    tail = ref[STATE:PAY, :].astype(F32)
    states = [ref[head(h), :].astype(F32) for h in range(HEADS)]
    factors = [tail[h : h + 1, 0:1] + tail[HEADS + h : HEADS + h + 1, 0:1] for h in range(HEADS)]
    return states, factors


def pick(flag, a, b):
    return jnp.where(flag, a, b)


def fold(outer, inner):
    (so, fo), (si, fi) = outer, inner
    return [so[h] + fo[h] * si[h] for h in range(HEADS)], [fo[h] * fi[h] for h in range(HEADS)]


def ordered(flag, a_ref, b_ref):
    (sa, fa), (sb, fb) = take(a_ref), take(b_ref)
    one = [pick(flag, p, q) for p, q in zip(sa, sb)], [pick(flag, p, q) for p, q in zip(fa, fb)]
    two = [pick(flag, q, p) for p, q in zip(sa, sb)], [pick(flag, q, p) for p, q in zip(fa, fb)]
    return one, two


def put(ref, folded):
    states, factors = folded
    for h in range(HEADS):
        ref[head(h), :] = states[h].astype(BF16)
    put_factors(ref, factors)


def chip_kernel(outer, at_ref, own_ref, other_ref, pay_ref):
    put(pay_ref, fold(*ordered(at_ref[4] == outer, own_ref, other_ref)))


def pair_kernel(a_ref, b_ref, pay_ref):
    put(pay_ref, fold(take(a_ref), take(b_ref)))


def entering(outer, at_ref, own_ref, other_ref, sibling_ref):
    states, _ = fold(*ordered(at_ref[4] == 0, own_ref, other_ref))
    near, factors = take(sibling_ref)
    return [pick(at_ref[4] == outer, near[h] + factors[h] * states[h], states[h]) for h in range(HEADS)]


def first_kernel(len_ref, at_ref, ld_ref, q_ref, k_ref, v_ref, pay_ref, local_ref):
    m = Masks(len_ref, at_ref, ld_ref)
    for h in range(HEADS):
        k, v = k_ref[:, head(h)], v_ref[:, head(h)]
        kept = (k.astype(F32) * m.keep(h)).astype(BF16)
        pay_ref[head(h), :] = dot(kept, v, TN).astype(BF16)
        attn = (dot(q_ref[:, head(h)], k, NT) * m.decay(h)).astype(BF16)
        local_ref[:, head(h)] = dot(attn, v, NN)
    put_factors(pay_ref, [m.through(h) for h in range(HEADS)])


def attend_kernel(len_ref, at_ref, ld_ref, q_ref, local_ref, a_ref, b_ref, c_ref, att_ref, state_ref):
    m = Masks(len_ref, at_ref, ld_ref)
    states = entering(1, at_ref, a_ref, b_ref, c_ref)
    for h in range(HEADS):
        state = states[h].astype(BF16)
        state_ref[head(h), :] = state
        carried = dot(q_ref[:, head(h)], state, NN) * m.enter(h)
        att_ref[:, head(h)] = (local_ref[:, head(h)] + carried).astype(BF16)


def back_kernel(len_ref, at_ref, ld_ref, q_ref, own_ref, other_ref, pay_ref, g_ref):
    m = Masks(len_ref, at_ref, ld_ref)
    for h in range(HEADS):
        g = (own_ref[:, head(h)] + other_ref[:, head(h)].astype(F32)).astype(BF16)
        g_ref[:, head(h)] = g
        entered = (q_ref[:, head(h)].astype(F32) * m.enter(h)).astype(BF16)
        pay_ref[head(h), :] = dot(entered, g, TN).astype(BF16)
    put_factors(pay_ref, [m.through(h) for h in range(HEADS)])


def grads_kernel(
    len_ref, at_ref, ld_ref, q_ref, k_ref, v_ref, g_ref, state_ref, a_ref, b_ref, c_ref, dq_ref, dk_ref, dv_ref
):
    m = Masks(len_ref, at_ref, ld_ref)
    carries = entering(0, at_ref, a_ref, b_ref, c_ref)
    for h in range(HEADS):
        q, k, v, g = (r[:, head(h)] for r in (q_ref, k_ref, v_ref, g_ref))
        decay, leave, carry = m.decay(h), m.leave(h), carries[h].astype(BF16)
        attn = (dot(q, k, NT) * decay).astype(BF16)
        back = (dot(g, v, NT) * decay).astype(BF16)
        dq = dot(back, k, NN) + dot(g, state_ref[head(h), :], NT) * m.enter(h)
        dk = dot(back, q, TN) + dot(v, carry, NT) * leave
        dv = dot(attn, g, TN) + dot(k, carry, NN) * leave
        dq_ref[:, head(h)] = dq.astype(BF16)
        dk_ref[:, head(h)] = dk.astype(BF16)
        dv_ref[:, head(h)] = dv.astype(BF16)


def chip_of(j, y, x, sign):
    far, near = j // 2, 2 * (j % 2)
    dy = lax.rem(sign * (far - y) + SIDE, SIDE)
    return dy, [lax.rem(sign * (near + e - x) + SIDE, SIDE) for e in range(2)]


def place(at_ref, along_y, along_x):
    flip = at_ref[4] == 0
    return pick(flip, along_y, along_x), pick(flip, along_x, along_y)


def weight_part(w_ref, j, at_ref):
    ry, rx = chip_of(j, at_ref[1], at_ref[2], -1)
    return jnp.concatenate([w_ref[place(at_ref, ry, r)] for r in rx], axis=0)


def pull_kernel(at_ref, g_ref, w_ref, own_ref, send_ref):
    total = jnp.zeros((2 * ROWS, STATE), F32)
    for j in range(LONG):
        total = total + dot(g_ref[j], weight_part(w_ref, j, at_ref), NN)
    own_ref[...] = total[:ROWS]
    send_ref[...] = total[ROWS:].astype(BF16)


def mix_kernel(at_ref, own_ref, other_ref, w_ref, out_ref):
    for j in range(LONG):
        w = weight_part(w_ref, j, at_ref)
        out_ref[j, :ROWS] = dot(own_ref[...], w, NT).astype(BF16)
        out_ref[j, ROWS:] = dot(other_ref[...], w, NT).astype(BF16)


def weight_grad_kernel(at_ref, g_ref, own_ref, other_ref, r_ref):
    for j in range(LONG):
        dy, dx = chip_of(j, at_ref[1], at_ref[2], 1)
        part = dot(g_ref[j, :ROWS], own_ref[...], TN) + dot(g_ref[j, ROWS:], other_ref[...], TN)
        part = part.astype(BF16)
        for e in range(2):
            rows = slice(e * HD, (e + 1) * HD)
            r_ref[place(at_ref, dy, dx[e])] = part[rows]


def ring(value, axis, steps):
    count = lax.axis_size(axis)
    return lax.ppermute(value, axis, [(i, (i + steps) % count) for i in range(count)])


SEQ = ("y", "x", "core")


def cross(value, axes, steps):
    pairs = []
    for y in range(SIDE):
        for x in range(SIDE):
            for c in range(2):
                up, on = ((y + steps) % SIDE, x) if axes[c] == "y" else (y, (x + steps) % SIDE)
                pairs.append(((y * SIDE + x) * 2 + c, (up * SIDE + on) * 2 + c))
    return lax.ppermute(value, SEQ, pairs)


def line(value, near, far):
    pairs = []
    for c, steps in enumerate((near, far)):
        pairs += [(2 * i + c, 2 * (i + steps) + c) for i in range(SIDE * SIDE) if 0 <= i + steps < SIDE * SIDE]
    return lax.ppermute(value, SEQ, pairs)


def gather_side(value, axes):
    return jnp.stack([value] + [cross(value, axes, s) for s in (1, 2, 3)])


def scatter_side(value, axes):
    parts = [value[0]] + [cross(value[s], axes, s) for s in (1, 2, 3)]
    return functools.reduce(jnp.add, [p.astype(F32) for p in parts])


def relay(at, pay, way, outer):
    sibling = swap(pay)
    [chip] = call(functools.partial(chip_kernel, outer), [((PAY, HD), BF16)], [SMEM] + [VMEM] * 2, 2**20)(
        at, pay, sibling
    )
    [share] = call(pair_kernel, [((PAY, HD), BF16)], [VMEM] * 2, 2**20)(
        line(chip, way, 3 * way), line(chip, 2 * way, 4 * way)
    )
    return share, swap(share), sibling


def swap(value):
    return ring(value, "core", 1)


def parity(value):
    return [jnp.concatenate([value[:, (2 * e + c) * HD : (2 * e + c + 1) * HD] for e in range(2)], 1) for c in range(2)]


def body(q, k, v, log_decay, lengths, weight, out_grad):
    y, x, c, z = (lax.axis_index(a) for a in ("y", "x", "core", "z"))
    at = jnp.stack([((y * SIDE + x) * 2 + c) * ROWS, y, x, z, c]).astype(jnp.int32)
    lead = (lengths, at, log_decay)
    lead_specs = [SMEM, SMEM, VMEM]
    even, odd = parity(out_grad)
    mine, yours = jnp.where(c == 0, even, odd), jnp.where(c == 0, odd, even)
    grads = lax.all_gather(jnp.concatenate([mine, swap(yours)], axis=0), "z")
    w = gather_side(gather_side(weight, "xy"), "yx")
    wide = ((ROWS, STATE), BF16)
    pay, local = call(
        first_kernel, [((PAY, HD), BF16), ((ROWS, STATE), F32)], lead_specs + [VMEM] * 3, 2**28
    )(*lead, q, k, v)
    att, state = call(attend_kernel, [wide, ((STATE, HD), BF16)], lead_specs + [VMEM] * 5, 2**26)(
        *lead, q, local, *relay(at, pay, 1, 1)
    )
    att_other = swap(att)
    [mixed] = call(mix_kernel, [((LONG, 2 * ROWS, HALF), BF16)], [SMEM] + [VMEM] * 3, 2**30)(
        at, att, att_other, w
    )
    mixed = lax.psum_scatter(mixed, "z", scatter_dimension=0)
    mixed_other = swap(mixed[ROWS:])
    mixed = mixed[:ROWS]
    even, odd = jnp.where(c == 0, mixed, mixed_other), jnp.where(c == 0, mixed_other, mixed)
    mixed = jnp.concatenate([even[:, :HD], odd[:, :HD], even[:, HD:], odd[:, HD:]], axis=1)
    own, send = call(pull_kernel, [((ROWS, STATE), F32), wide], [SMEM] + [VMEM] * 2, 2**30)(at, grads, w)
    back, g = call(back_kernel, [((PAY, HD), BF16), wide], lead_specs + [VMEM] * 3, 2**26)(
        *lead, q, own, swap(send)
    )
    grid = ((SIDE, SIDE, HD, STATE), BF16)
    [r] = call(weight_grad_kernel, [grid], [SMEM] + [VMEM] * 3, 2**30)(at, grads, att, att_other)
    r = scatter_side(scatter_side(r, "yx").astype(BF16), "xy")
    dq, dk, dv = call(grads_kernel, [wide] * 3, lead_specs + [VMEM] * 8, 2**29)(
        *lead, q, k, v, g, state, *relay(at, back, -1, 0)
    )
    return mixed, dq, dk, dv, r


def solution(mesh):
    fine = Mesh(mesh.devices.reshape(SIDE, SIDE, 2, LONG), ("y", "x", "core", "z"))
    seq = ("y", "x", "core")
    wide = P(seq, "z")
    return jax.shard_map(
        body,
        mesh=fine,
        in_specs=(wide, wide, wide, P("z", seq), P(), wide, wide),
        out_specs=(wide,) * 5,
        check_vma=False,
    )
```

```python
import functools

import jax
import jax.numpy as jnp
from jax import lax
from jax.experimental import pallas as pl
from jax.experimental.pallas import tpu as pltpu
from jax.sharding import Mesh, PartitionSpec as P

F32 = jnp.float32
BF16 = jnp.bfloat16
HIGH = lax.Precision.HIGHEST
SIDE = 4
LONG = 8
HEADS = 4
HD = 128
ROWS = 256
HALF = 256
STATE = HEADS * HD
PAY = STATE + 16
DOCS = 16
VMEM = pl.BlockSpec(memory_space=pltpu.VMEM)
SMEM = pl.BlockSpec(memory_space=pltpu.SMEM)


def call(kernel, outs, specs, us, after=()):
    gates = len(after)
    made = pl.pallas_call(
        lambda *refs: kernel(*refs[gates:]),
        out_shape=[jax.ShapeDtypeStruct(s, d) for s, d in outs],
        in_specs=[pl.BlockSpec(memory_space=pl.ANY)] * gates + specs,
        out_specs=[VMEM] * len(outs),
        compiler_params=pltpu.CompilerParams(vmem_limit_bytes=48 * 2**20),
        cost_estimate=pl.CostEstimate(flops=int(us * 3 * 10**9), bytes_accessed=2**20, transcendentals=0),
    )
    return lambda *args: made(*after, *args)


def dot(a, b, dims, precision=None):
    return lax.dot_general(a, b, (dims, ((), ())), precision=precision, preferred_element_type=F32)


NN = ((1,), (0,))
NT = ((1,), (1,))
TN = ((0,), (0,))


class Masks:
    def __init__(self, len_ref, at_ref, ld_ref):
        first = at_ref[0]
        pos_r = first + lax.broadcasted_iota(jnp.int32, (1, ROWS), 1)
        pos_c = first + lax.broadcasted_iota(jnp.int32, (ROWS, 1), 0)
        doc_r = jnp.full((1, ROWS), -1, jnp.int32)
        doc_c = jnp.full((ROWS, 1), -1, jnp.int32)
        edge = [jnp.int32(-1)] * 3
        start = jnp.int32(0)
        for j in range(DOCS):
            doc_r = doc_r + jnp.where(pos_r >= start, 1, 0)
            doc_c = doc_c + jnp.where(pos_c >= start, 1, 0)
            for n, p in enumerate((first - 1, first + ROWS - 1, first + ROWS)):
                edge[n] = edge[n] + jnp.where(p >= start, 1, 0)
            start = start + len_ref[j]
        prev, last, after = edge
        row = lax.broadcasted_iota(jnp.int32, (ROWS, ROWS), 0)
        col = lax.broadcasted_iota(jnp.int32, (ROWS, ROWS), 1)
        ld = ld_ref[...]
        self.cum_r = dot(ld, jnp.where(row <= col, 1.0, 0.0).astype(F32), NN, HIGH)
        self.cum_c = dot(jnp.where(col <= row, 1.0, 0.0).astype(F32), ld, NT, HIGH)
        self.joint = jnp.logical_and(row >= col, doc_c == doc_r)
        self.first_doc, self.last_doc, self.next_doc = doc_c == prev, doc_c == last, doc_c == after
        self.whole = prev == last

    def decay(self, h):
        gap = self.cum_c[:, h : h + 1] - self.cum_r[h : h + 1, :]
        return jnp.where(self.joint, jnp.exp(jnp.where(self.joint, gap, 0.0)), 0.0)

    def total(self, h):
        return self.cum_r[h : h + 1, ROWS - 1 : ROWS]

    def enter(self, h):
        return jnp.where(self.first_doc, jnp.exp(self.cum_c[:, h : h + 1]), 0.0)

    def tail(self, h):
        return jnp.exp(self.total(h) - self.cum_c[:, h : h + 1])

    def keep(self, h):
        return jnp.where(self.last_doc, self.tail(h), 0.0)

    def leave(self, h):
        return jnp.where(self.next_doc, self.tail(h), 0.0)

    def through(self, h):
        return jnp.where(self.whole, jnp.exp(self.total(h)), 0.0)


def head(h):
    return slice(h * HD, (h + 1) * HD)


def put_factors(ref, factors):
    row = lax.broadcasted_iota(jnp.int32, (16, HD), 0)
    block = jnp.zeros((16, HD), F32)
    for h, f in enumerate(factors):
        high = f.astype(BF16).astype(F32)
        block = block + jnp.where(row == h, high, 0.0) + jnp.where(row == HEADS + h, f - high, 0.0)
    ref[STATE:PAY, :] = block.astype(BF16)


def take(ref):
    tail = ref[STATE:PAY, :].astype(F32)
    states = [ref[head(h), :].astype(F32) for h in range(HEADS)]
    factors = [tail[h : h + 1, 0:1] + tail[HEADS + h : HEADS + h + 1, 0:1] for h in range(HEADS)]
    return states, factors


def pick(flag, a, b):
    return jnp.where(flag, a, b)


def fold(outer, inner):
    (so, fo), (si, fi) = outer, inner
    return [so[h] + fo[h] * si[h] for h in range(HEADS)], [fo[h] * fi[h] for h in range(HEADS)]


def ordered(flag, a_ref, b_ref):
    (sa, fa), (sb, fb) = take(a_ref), take(b_ref)
    one = [pick(flag, p, q) for p, q in zip(sa, sb)], [pick(flag, p, q) for p, q in zip(fa, fb)]
    two = [pick(flag, q, p) for p, q in zip(sa, sb)], [pick(flag, q, p) for p, q in zip(fa, fb)]
    return one, two


def put(ref, folded):
    states, factors = folded
    for h in range(HEADS):
        ref[head(h), :] = states[h].astype(BF16)
    put_factors(ref, factors)


def chip_kernel(outer, at_ref, own_ref, other_ref, pay_ref):
    put(pay_ref, fold(*ordered(at_ref[4] == outer, own_ref, other_ref)))


def pair_kernel(a_ref, b_ref, pay_ref):
    put(pay_ref, fold(take(a_ref), take(b_ref)))


def entering(outer, at_ref, own_ref, other_ref, sibling_ref):
    states, _ = fold(*ordered(at_ref[4] == 0, own_ref, other_ref))
    near, factors = take(sibling_ref)
    return [pick(at_ref[4] == outer, near[h] + factors[h] * states[h], states[h]) for h in range(HEADS)]


def first_kernel(len_ref, at_ref, ld_ref, q_ref, k_ref, v_ref, pay_ref, local_ref):
    m = Masks(len_ref, at_ref, ld_ref)
    for h in range(HEADS):
        k, v = k_ref[:, head(h)], v_ref[:, head(h)]
        kept = (k.astype(F32) * m.keep(h)).astype(BF16)
        pay_ref[head(h), :] = dot(kept, v, TN).astype(BF16)
        attn = (dot(q_ref[:, head(h)], k, NT) * m.decay(h)).astype(BF16)
        local_ref[:, head(h)] = dot(attn, v, NN)
    put_factors(pay_ref, [m.through(h) for h in range(HEADS)])


def attend_kernel(len_ref, at_ref, ld_ref, q_ref, local_ref, a_ref, b_ref, c_ref, att_ref, state_ref):
    m = Masks(len_ref, at_ref, ld_ref)
    states = entering(1, at_ref, a_ref, b_ref, c_ref)
    for h in range(HEADS):
        state = states[h].astype(BF16)
        state_ref[head(h), :] = state
        carried = dot(q_ref[:, head(h)], state, NN) * m.enter(h)
        att_ref[:, head(h)] = (local_ref[:, head(h)] + carried).astype(BF16)


def back_kernel(len_ref, at_ref, ld_ref, q_ref, own_ref, other_ref, pay_ref, g_ref):
    m = Masks(len_ref, at_ref, ld_ref)
    for h in range(HEADS):
        g = (own_ref[:, head(h)] + other_ref[:, head(h)].astype(F32)).astype(BF16)
        g_ref[:, head(h)] = g
        entered = (q_ref[:, head(h)].astype(F32) * m.enter(h)).astype(BF16)
        pay_ref[head(h), :] = dot(entered, g, TN).astype(BF16)
    put_factors(pay_ref, [m.through(h) for h in range(HEADS)])


def grads_kernel(
    len_ref, at_ref, ld_ref, q_ref, k_ref, v_ref, g_ref, state_ref, a_ref, b_ref, c_ref, dq_ref, dk_ref, dv_ref
):
    m = Masks(len_ref, at_ref, ld_ref)
    carries = entering(0, at_ref, a_ref, b_ref, c_ref)
    for h in range(HEADS):
        q, k, v, g = (r[:, head(h)] for r in (q_ref, k_ref, v_ref, g_ref))
        decay, leave, carry = m.decay(h), m.leave(h), carries[h].astype(BF16)
        attn = (dot(q, k, NT) * decay).astype(BF16)
        back = (dot(g, v, NT) * decay).astype(BF16)
        dq = dot(back, k, NN) + dot(g, state_ref[head(h), :], NT) * m.enter(h)
        dk = dot(back, q, TN) + dot(v, carry, NT) * leave
        dv = dot(attn, g, TN) + dot(k, carry, NN) * leave
        dq_ref[:, head(h)] = dq.astype(BF16)
        dk_ref[:, head(h)] = dk.astype(BF16)
        dv_ref[:, head(h)] = dv.astype(BF16)


def chip_of(j, y, x, sign):
    far, near = j // 2, 2 * (j % 2)
    dy = lax.rem(sign * (far - y) + SIDE, SIDE)
    return dy, [lax.rem(sign * (near + e - x) + SIDE, SIDE) for e in range(2)]


def place(at_ref, along_y, along_x):
    flip = at_ref[4] == 0
    return pick(flip, along_y, along_x), pick(flip, along_x, along_y)


def weight_part(w_ref, j, at_ref):
    ry, rx = chip_of(j, at_ref[1], at_ref[2], -1)
    return jnp.concatenate([w_ref[place(at_ref, ry, r)] for r in rx], axis=0)


def pull_kernel(at_ref, w_ref, *refs):
    g_refs, (own_ref, send_ref) = refs[:LONG], refs[LONG:]
    total = jnp.zeros((2 * ROWS, STATE), F32)
    for s, g_ref in enumerate(g_refs):
        j = lax.rem(at_ref[3] - s + LONG, LONG)
        total = total + dot(g_ref[...], weight_part(w_ref, j, at_ref), NN)
    own_ref[...] = total[:ROWS]
    send_ref[...] = total[ROWS:].astype(BF16)


def mix_kernel(at_ref, own_ref, other_ref, w_ref, *out_refs):
    for s, out_ref in enumerate(out_refs):
        w = weight_part(w_ref, lax.rem(at_ref[3] + s, LONG), at_ref)
        out_ref[:ROWS] = dot(own_ref[...], w, NT).astype(BF16)
        out_ref[ROWS:] = dot(other_ref[...], w, NT).astype(BF16)


def weight_grad_kernel(at_ref, own_ref, other_ref, *refs):
    g_refs, r_ref = refs[:LONG], refs[LONG]
    for s, g_ref in enumerate(g_refs):
        j = lax.rem(at_ref[3] - s + LONG, LONG)
        dy, dx = chip_of(j, at_ref[1], at_ref[2], 1)
        part = dot(g_ref[:ROWS], own_ref[...], TN) + dot(g_ref[ROWS:], other_ref[...], TN)
        part = part.astype(BF16)
        for e in range(2):
            r_ref[place(at_ref, dy, dx[e])] = part[e * HD : (e + 1) * HD]


def ring(value, axis, steps):
    count = lax.axis_size(axis)
    return lax.ppermute(value, axis, [(i, (i + steps) % count) for i in range(count)])


SEQ = ("y", "x", "core")


def cross(value, axes, steps):
    pairs = []
    for y in range(SIDE):
        for x in range(SIDE):
            for c in range(2):
                up, on = ((y + steps) % SIDE, x) if axes[c] == "y" else (y, (x + steps) % SIDE)
                pairs.append(((y * SIDE + x) * 2 + c, (up * SIDE + on) * 2 + c))
    return lax.ppermute(value, SEQ, pairs)


def line(value, near, far):
    pairs = []
    for c, steps in enumerate((near, far)):
        pairs += [(2 * i + c, 2 * (i + steps) + c) for i in range(SIDE * SIDE) if 0 <= i + steps < SIDE * SIDE]
    return lax.ppermute(value, SEQ, pairs)


def stack_kernel(*refs):
    for n, ref in enumerate(refs[:-1]):
        refs[-1][n] = ref[...]


def gather_side(value, axes, after=()):
    parts = [value] + [cross(value, axes, s) for s in (1, 2, 3)]
    return call(stack_kernel, [((SIDE,) + value.shape, BF16)], [VMEM] * SIDE, 0.7, after)(*parts)[0]


def scatter_side(value, axes):
    parts = [value[0]] + [cross(value[s], axes, s) for s in (1, 2, 3)]
    return functools.reduce(jnp.add, [p.astype(F32) for p in parts])


def relay(at, pay, way, outer, chip_after, pair_after):
    sibling = swap(pay)
    [chip] = call(functools.partial(chip_kernel, outer), [((PAY, HD), BF16)], [SMEM] + [VMEM] * 2, 0.7, chip_after)(
        at, pay, sibling
    )
    [share] = call(pair_kernel, [((PAY, HD), BF16)], [VMEM] * 2, 0.7, pair_after)(
        line(chip, way, 3 * way), line(chip, 2 * way, 4 * way)
    )
    return share, swap(share), sibling


def long_cross(value, steps):
    pairs = [(c * LONG + z, c * LONG + (z + (1 - 2 * c) * steps) % LONG) for c in range(2) for z in range(LONG)]
    return lax.ppermute(value, ("core", "z"), pairs)


def gather_long(value, even):
    parts = [None] * LONG
    parts[0] = right = left = value
    for s in range(1, LONG // 2):
        parts[s] = right = ring(right, "z", 1)
        parts[LONG - s] = left = ring(left, "z", -1)
    parts[LONG // 2] = long_cross(jnp.where(even, right, left), 1)
    return parts


def add(a, b):
    return (a.astype(F32) + b.astype(F32)).astype(BF16)


def scatter_long(value, even):
    half = LONG // 2
    far = long_cross(value[half], 1)
    right = jnp.where(even, add(value[half - 1], far), value[half - 1])
    left = jnp.where(even, value[half + 1], add(value[half + 1], far))
    stages = [(right, left)]
    for s in range(1, half - 1):
        right = add(value[half - 1 - s], ring(right, "z", 1))
        left = add(value[half + 1 + s], ring(left, "z", -1))
        stages.append((right, left))
    right, left = ring(right, "z", 1), ring(left, "z", -1)
    return (value[0].astype(F32) + right.astype(F32) + left.astype(F32)).astype(BF16), stages


def swap(value):
    return ring(value, "core", 1)


def parity(value):
    return [jnp.concatenate([value[:, (2 * e + c) * HD : (2 * e + c + 1) * HD] for e in range(2)], 1) for c in range(2)]


def body(q, k, v, log_decay, lengths, weight, out_grad):
    y, x, c, z = (lax.axis_index(a) for a in ("y", "x", "core", "z"))
    at = jnp.stack([((y * SIDE + x) * 2 + c) * ROWS, y, x, z, c]).astype(jnp.int32)
    lead = (lengths, at, log_decay)
    lead_specs = [SMEM, SMEM, VMEM]
    even, odd = parity(out_grad)
    mine, yours = jnp.where(c == 0, even, odd), jnp.where(c == 0, odd, even)
    grads = gather_long(jnp.concatenate([mine, swap(yours)], axis=0), c == 0)
    near = gather_side(weight, "xy", (grads[1], grads[7]))
    w = gather_side(near, "yx")
    first_after = (near,)
    wide = ((ROWS, STATE), BF16)
    pay, local = call(
        first_kernel, [((PAY, HD), BF16), ((ROWS, STATE), F32)], lead_specs + [VMEM] * 3, 2.3, first_after
    )(*lead, q, k, v)
    att, state = call(attend_kernel, [wide, ((STATE, HD), BF16)], lead_specs + [VMEM] * 5, 1.9)(
        *lead, q, local, *relay(at, pay, 1, 1, (grads[2], grads[6]), (grads[3], grads[5]))
    )
    att_other = swap(att)
    mixed = call(mix_kernel, [((2 * ROWS, HALF), BF16)] * LONG, [SMEM] + [VMEM] * 3, 1.9, (grads[4],))(
        at, att, att_other, w
    )
    mixed, stages = scatter_long(mixed, c == 0)
    mixed_other = swap(mixed[ROWS:])
    mixed = mixed[:ROWS]
    even, odd = jnp.where(c == 0, mixed, mixed_other), jnp.where(c == 0, mixed_other, mixed)
    mixed = jnp.concatenate([even[:, :HD], odd[:, :HD], even[:, HD:], odd[:, HD:]], axis=1)
    own, send = call(pull_kernel, [((ROWS, STATE), F32), wide], [SMEM] + [VMEM] * (1 + LONG), 1.9)(at, w, *grads)
    back, g = call(back_kernel, [((PAY, HD), BF16), wide], lead_specs + [VMEM] * 3, 1.6)(
        *lead, q, own, swap(send)
    )
    grid = ((SIDE, SIDE, HD, STATE), BF16)
    [r] = call(weight_grad_kernel, [grid], [SMEM] + [VMEM] * (2 + LONG), 1.9)(
        at, att, att_other, *grads
    )
    r_near = scatter_side(r, "yx").astype(BF16)
    r = scatter_side(r_near, "xy")
    dq, dk, dv = call(grads_kernel, [wide] * 3, lead_specs + [VMEM] * 8, 3.3, (r_near, *stages[2]))(
        *lead, q, k, v, g, state, *relay(at, back, -1, 0, stages[0], stages[1])
    )
    return mixed, dq, dk, dv, r


def solution(mesh):
    fine = Mesh(mesh.devices.reshape(SIDE, SIDE, 2, LONG), ("y", "x", "core", "z"))
    seq = ("y", "x", "core")
    wide = P(seq, "z")
    return jax.shard_map(
        body,
        mesh=fine,
        in_specs=(wide, wide, wide, P("z", seq), P(), wide, wide),
        out_specs=(wide,) * 5,
        check_vma=False,
    )
```

```python
import functools

import jax
import jax.numpy as jnp
from jax import lax
from jax.experimental import pallas as pl
from jax.experimental.pallas import tpu as pltpu
from jax.sharding import Mesh, PartitionSpec as P

F32 = jnp.float32
BF16 = jnp.bfloat16
HIGH = lax.Precision.HIGHEST
SIDE = 4
LONG = 8
HEADS = 4
HD = 128
ROWS = 256
HALF = 256
STATE = HEADS * HD
PAY = STATE + 16
DOCS = 16
VMEM = pl.BlockSpec(memory_space=pltpu.VMEM)
SMEM = pl.BlockSpec(memory_space=pltpu.SMEM)


def call(kernel, outs, specs, us, after=()):
    gates = len(after)
    made = pl.pallas_call(
        lambda *refs: kernel(*refs[gates:]),
        out_shape=[jax.ShapeDtypeStruct(s, d) for s, d in outs],
        in_specs=[pl.BlockSpec(memory_space=pl.ANY)] * gates + specs,
        out_specs=[VMEM] * len(outs),
        compiler_params=pltpu.CompilerParams(vmem_limit_bytes=48 * 2**20),
        cost_estimate=pl.CostEstimate(flops=int(us * 3 * 10**9), bytes_accessed=2**20, transcendentals=0),
    )
    return lambda *args: made(*after, *args)


def dot(a, b, dims, precision=None):
    return lax.dot_general(a, b, (dims, ((), ())), precision=precision, preferred_element_type=F32)


NN = ((1,), (0,))
NT = ((1,), (1,))
TN = ((0,), (0,))


class Masks:
    def __init__(self, len_ref, at_ref, ld_ref):
        first = at_ref[0]
        pos_r = first + lax.broadcasted_iota(jnp.int32, (1, ROWS), 1)
        pos_c = first + lax.broadcasted_iota(jnp.int32, (ROWS, 1), 0)
        doc_r = jnp.full((1, ROWS), -1, jnp.int32)
        doc_c = jnp.full((ROWS, 1), -1, jnp.int32)
        edge = [jnp.int32(-1)] * 3
        start = jnp.int32(0)
        for j in range(DOCS):
            doc_r = doc_r + jnp.where(pos_r >= start, 1, 0)
            doc_c = doc_c + jnp.where(pos_c >= start, 1, 0)
            for n, p in enumerate((first - 1, first + ROWS - 1, first + ROWS)):
                edge[n] = edge[n] + jnp.where(p >= start, 1, 0)
            start = start + len_ref[j]
        prev, last, after = edge
        row = lax.broadcasted_iota(jnp.int32, (ROWS, ROWS), 0)
        col = lax.broadcasted_iota(jnp.int32, (ROWS, ROWS), 1)
        ld = ld_ref[...]
        self.cum_r = dot(ld, jnp.where(row <= col, 1.0, 0.0).astype(F32), NN, HIGH)
        self.cum_c = dot(jnp.where(col <= row, 1.0, 0.0).astype(F32), ld, NT, HIGH)
        self.joint = jnp.logical_and(row >= col, doc_c == doc_r)
        self.first_doc, self.last_doc, self.next_doc = doc_c == prev, doc_c == last, doc_c == after
        self.whole = prev == last

    def decay(self, h):
        gap = self.cum_c[:, h : h + 1] - self.cum_r[h : h + 1, :]
        return jnp.where(self.joint, jnp.exp(jnp.where(self.joint, gap, 0.0)), 0.0)

    def total(self, h):
        return self.cum_r[h : h + 1, ROWS - 1 : ROWS]

    def enter(self, h):
        return jnp.where(self.first_doc, jnp.exp(self.cum_c[:, h : h + 1]), 0.0)

    def tail(self, h):
        return jnp.exp(self.total(h) - self.cum_c[:, h : h + 1])

    def keep(self, h):
        return jnp.where(self.last_doc, self.tail(h), 0.0)

    def leave(self, h):
        return jnp.where(self.next_doc, self.tail(h), 0.0)

    def through(self, h):
        return jnp.where(self.whole, jnp.exp(self.total(h)), 0.0)


def head(h):
    return slice(h * HD, (h + 1) * HD)


def put_factors(ref, factors):
    row = lax.broadcasted_iota(jnp.int32, (16, HD), 0)
    block = jnp.zeros((16, HD), F32)
    for h, f in enumerate(factors):
        high = f.astype(BF16).astype(F32)
        block = block + jnp.where(row == h, high, 0.0) + jnp.where(row == HEADS + h, f - high, 0.0)
    ref[STATE:PAY, :] = block.astype(BF16)


def take(ref):
    tail = ref[STATE:PAY, :].astype(F32)
    states = [ref[head(h), :].astype(F32) for h in range(HEADS)]
    factors = [tail[h : h + 1, 0:1] + tail[HEADS + h : HEADS + h + 1, 0:1] for h in range(HEADS)]
    return states, factors


def pick(flag, a, b):
    return jnp.where(flag, a, b)


def fold(outer, inner):
    (so, fo), (si, fi) = outer, inner
    return [so[h] + fo[h] * si[h] for h in range(HEADS)], [fo[h] * fi[h] for h in range(HEADS)]


def ordered(flag, a_ref, b_ref):
    (sa, fa), (sb, fb) = take(a_ref), take(b_ref)
    one = [pick(flag, p, q) for p, q in zip(sa, sb)], [pick(flag, p, q) for p, q in zip(fa, fb)]
    two = [pick(flag, q, p) for p, q in zip(sa, sb)], [pick(flag, q, p) for p, q in zip(fa, fb)]
    return one, two


def put(ref, folded):
    states, factors = folded
    for h in range(HEADS):
        ref[head(h), :] = states[h].astype(BF16)
    put_factors(ref, factors)


def chip_kernel(outer, at_ref, own_ref, other_ref, pay_ref):
    put(pay_ref, fold(*ordered(at_ref[4] == outer, own_ref, other_ref)))


def pair_kernel(a_ref, b_ref, pay_ref):
    put(pay_ref, fold(take(a_ref), take(b_ref)))


def entering(outer, at_ref, own_ref, other_ref, sibling_ref):
    states, _ = fold(*ordered(at_ref[4] == 0, own_ref, other_ref))
    near, factors = take(sibling_ref)
    return [pick(at_ref[4] == outer, near[h] + factors[h] * states[h], states[h]) for h in range(HEADS)]


def first_kernel(len_ref, at_ref, ld_ref, q_ref, k_ref, v_ref, pay_ref, local_ref):
    m = Masks(len_ref, at_ref, ld_ref)
    for h in range(HEADS):
        k, v = k_ref[:, head(h)], v_ref[:, head(h)]
        kept = (k.astype(F32) * m.keep(h)).astype(BF16)
        pay_ref[head(h), :] = dot(kept, v, TN).astype(BF16)
        attn = (dot(q_ref[:, head(h)], k, NT) * m.decay(h)).astype(BF16)
        local_ref[:, head(h)] = dot(attn, v, NN)
    put_factors(pay_ref, [m.through(h) for h in range(HEADS)])


def attend_kernel(len_ref, at_ref, ld_ref, q_ref, local_ref, a_ref, b_ref, c_ref, att_ref, state_ref):
    m = Masks(len_ref, at_ref, ld_ref)
    states = entering(1, at_ref, a_ref, b_ref, c_ref)
    for h in range(HEADS):
        state = states[h].astype(BF16)
        state_ref[head(h), :] = state
        carried = dot(q_ref[:, head(h)], state, NN) * m.enter(h)
        att_ref[:, head(h)] = (local_ref[:, head(h)] + carried).astype(BF16)


def back_kernel(len_ref, at_ref, ld_ref, q_ref, own_ref, other_ref, pay_ref, g_ref):
    m = Masks(len_ref, at_ref, ld_ref)
    for h in range(HEADS):
        g = (own_ref[:, head(h)] + other_ref[:, head(h)].astype(F32)).astype(BF16)
        g_ref[:, head(h)] = g
        entered = (q_ref[:, head(h)].astype(F32) * m.enter(h)).astype(BF16)
        pay_ref[head(h), :] = dot(entered, g, TN).astype(BF16)
    put_factors(pay_ref, [m.through(h) for h in range(HEADS)])


def grads_kernel(
    len_ref, at_ref, ld_ref, q_ref, k_ref, v_ref, g_ref, state_ref, a_ref, b_ref, c_ref, dq_ref, dk_ref, dv_ref
):
    m = Masks(len_ref, at_ref, ld_ref)
    carries = entering(0, at_ref, a_ref, b_ref, c_ref)
    for h in range(HEADS):
        q, k, v, g = (r[:, head(h)] for r in (q_ref, k_ref, v_ref, g_ref))
        decay, leave, carry = m.decay(h), m.leave(h), carries[h].astype(BF16)
        attn = (dot(q, k, NT) * decay).astype(BF16)
        back = (dot(g, v, NT) * decay).astype(BF16)
        dq = dot(back, k, NN) + dot(g, state_ref[head(h), :], NT) * m.enter(h)
        dk = dot(back, q, TN) + dot(v, carry, NT) * leave
        dv = dot(attn, g, TN) + dot(k, carry, NN) * leave
        dq_ref[:, head(h)] = dq.astype(BF16)
        dk_ref[:, head(h)] = dk.astype(BF16)
        dv_ref[:, head(h)] = dv.astype(BF16)


def chip_of(j, y, x, sign):
    far, near = j // 2, 2 * (j % 2)
    dy = lax.rem(sign * (far - y) + SIDE, SIDE)
    return dy, [lax.rem(sign * (near + e - x) + SIDE, SIDE) for e in range(2)]


def place(at_ref, along_y, along_x):
    flip = at_ref[4] == 0
    return pick(flip, along_y, along_x), pick(flip, along_x, along_y)


def weight_part(w_ref, j, at_ref):
    ry, rx = chip_of(j, at_ref[1], at_ref[2], -1)
    return jnp.concatenate([w_ref[place(at_ref, ry, r)] for r in rx], axis=0)


def pull_kernel(at_ref, w_ref, *refs):
    g_refs, (own_ref, send_ref) = refs[:LONG], refs[LONG:]
    total = jnp.zeros((2 * ROWS, STATE), F32)
    for s, g_ref in enumerate(g_refs):
        j = lax.rem(at_ref[3] - s + LONG, LONG)
        total = total + dot(g_ref[...], weight_part(w_ref, j, at_ref), NN)
    own_ref[...] = total[:ROWS]
    send_ref[...] = total[ROWS:].astype(BF16)


def mix_kernel(at_ref, own_ref, other_ref, w_ref, *out_refs):
    for s, out_ref in enumerate(out_refs):
        w = weight_part(w_ref, lax.rem(at_ref[3] + s, LONG), at_ref)
        out_ref[:ROWS] = dot(own_ref[...], w, NT).astype(BF16)
        out_ref[ROWS:] = dot(other_ref[...], w, NT).astype(BF16)


def weight_grad_kernel(at_ref, own_ref, other_ref, *refs):
    g_refs, r_ref = refs[:LONG], refs[LONG]
    for s, g_ref in enumerate(g_refs):
        j = lax.rem(at_ref[3] - s + LONG, LONG)
        dy, dx = chip_of(j, at_ref[1], at_ref[2], 1)
        part = dot(g_ref[:ROWS], own_ref[...], TN) + dot(g_ref[ROWS:], other_ref[...], TN)
        part = part.astype(BF16)
        for e in range(2):
            r_ref[place(at_ref, dy, dx[e])] = part[e * HD : (e + 1) * HD]


def ring(value, axis, steps):
    count = lax.axis_size(axis)
    return lax.ppermute(value, axis, [(i, (i + steps) % count) for i in range(count)])


SEQ = ("y", "x", "core")


def cross(value, axes, steps):
    pairs = []
    for y in range(SIDE):
        for x in range(SIDE):
            for c in range(2):
                up, on = ((y + steps) % SIDE, x) if axes[c] == "y" else (y, (x + steps) % SIDE)
                pairs.append(((y * SIDE + x) * 2 + c, (up * SIDE + on) * 2 + c))
    return lax.ppermute(value, SEQ, pairs)


def line(value, near, far):
    pairs = []
    for c, steps in enumerate((near, far)):
        pairs += [(2 * i + c, 2 * (i + steps) + c) for i in range(SIDE * SIDE) if 0 <= i + steps < SIDE * SIDE]
    return lax.ppermute(value, SEQ, pairs)


def stack_kernel(*refs):
    for n, ref in enumerate(refs[:-1]):
        refs[-1][n] = ref[...]


def gather_side(value, axes, after=()):
    parts = [value] + [cross(value, axes, s) for s in (1, 2, 3)]
    return call(stack_kernel, [((SIDE,) + value.shape, BF16)], [VMEM] * SIDE, 0.7, after)(*parts)[0]


def scatter_side(value, axes):
    parts = [value[0]] + [cross(value[s], axes, s) for s in (1, 2, 3)]
    return functools.reduce(jnp.add, [p.astype(F32) for p in parts])


def relay(at, pay, way, outer, chip_after, pair_after):
    sibling = swap(pay)
    [chip] = call(functools.partial(chip_kernel, outer), [((PAY, HD), BF16)], [SMEM] + [VMEM] * 2, 0.7, chip_after)(
        at, pay, sibling
    )
    [share] = call(pair_kernel, [((PAY, HD), BF16)], [VMEM] * 2, 0.7, pair_after)(
        line(chip, way, 3 * way), line(chip, 2 * way, 4 * way)
    )
    return share, swap(share), sibling


def long_cross(value, steps):
    pairs = [(c * LONG + z, c * LONG + (z + (1 - 2 * c) * steps) % LONG) for c in range(2) for z in range(LONG)]
    return lax.ppermute(value, ("core", "z"), pairs)


def gather_long(value, even):
    parts = [None] * LONG
    parts[0] = right = left = value
    for s in range(1, LONG // 2):
        parts[s] = right = ring(right, "z", 1)
        parts[LONG - s] = left = ring(left, "z", -1)
    parts[LONG // 2] = long_cross(jnp.where(even, right, left), 1)
    return parts


def add(a, b):
    return (a.astype(F32) + b.astype(F32)).astype(BF16)


def scatter_long(value, even):
    half = LONG // 2
    far = long_cross(value[half], 1)
    right = jnp.where(even, add(value[half - 1], far), value[half - 1])
    left = jnp.where(even, value[half + 1], add(value[half + 1], far))
    stages = [(right, left)]
    for s in range(1, half - 1):
        right = add(value[half - 1 - s], ring(right, "z", 1))
        left = add(value[half + 1 + s], ring(left, "z", -1))
        stages.append((right, left))
    return (value[0], ring(right, "z", 1), ring(left, "z", -1)), stages


def sum_kernel(one_ref, two_ref, three_ref, out_ref):
    total = one_ref[...].astype(F32) + two_ref[...].astype(F32) + three_ref[...].astype(F32)
    out_ref[...] = total.astype(BF16)


def swap(value):
    return ring(value, "core", 1)


def parity(value):
    return [jnp.concatenate([value[:, (2 * e + c) * HD : (2 * e + c + 1) * HD] for e in range(2)], 1) for c in range(2)]


def body(q, k, v, log_decay, lengths, weight, out_grad):
    y, x, c, z = (lax.axis_index(a) for a in ("y", "x", "core", "z"))
    at = jnp.stack([((y * SIDE + x) * 2 + c) * ROWS, y, x, z, c]).astype(jnp.int32)
    lead = (lengths, at, log_decay)
    lead_specs = [SMEM, SMEM, VMEM]
    even, odd = parity(out_grad)
    mine, yours = jnp.where(c == 0, even, odd), jnp.where(c == 0, odd, even)
    grads = gather_long(jnp.concatenate([mine, swap(yours)], axis=0), c == 0)
    near = gather_side(weight, "xy", (grads[1], grads[7]))
    w = gather_side(near, "yx")
    first_after = (near,)
    wide = ((ROWS, STATE), BF16)
    pay, local = call(
        first_kernel, [((PAY, HD), BF16), ((ROWS, STATE), F32)], lead_specs + [VMEM] * 3, 2.3, first_after
    )(*lead, q, k, v)
    att, state = call(attend_kernel, [wide, ((STATE, HD), BF16)], lead_specs + [VMEM] * 5, 1.9)(
        *lead, q, local, *relay(at, pay, 1, 1, (grads[2], grads[6]), (grads[3], grads[5]))
    )
    att_other = swap(att)
    mixed = call(mix_kernel, [((2 * ROWS, HALF), BF16)] * LONG, [SMEM] + [VMEM] * 3, 1.9, (grads[4],))(
        at, att, att_other, w
    )
    shares, stages = scatter_long(mixed, c == 0)
    own, send = call(pull_kernel, [((ROWS, STATE), F32), wide], [SMEM] + [VMEM] * (1 + LONG), 1.9)(at, w, *grads)
    back, g = call(back_kernel, [((PAY, HD), BF16), wide], lead_specs + [VMEM] * 3, 1.6)(
        *lead, q, own, swap(send)
    )
    grid = ((SIDE, SIDE, HD, STATE), BF16)
    [r] = call(weight_grad_kernel, [grid], [SMEM] + [VMEM] * (2 + LONG), 1.9)(
        at, att, att_other, *grads
    )
    r_near = scatter_side(r, "yx").astype(BF16)
    r = scatter_side(r_near, "xy")
    dq, dk, dv = call(grads_kernel, [wide] * 3, lead_specs + [VMEM] * 8, 3.3, (*stages[2],))(
        *lead, q, k, v, g, state, *relay(at, back, -1, 0, stages[0], stages[1])
    )
    [mixed] = call(sum_kernel, [((2 * ROWS, HALF), BF16)], [VMEM] * 3, 0.5, (dq,))(*shares)
    mixed_other = swap(mixed[ROWS:])
    mixed = mixed[:ROWS]
    even, odd = jnp.where(c == 0, mixed, mixed_other), jnp.where(c == 0, mixed_other, mixed)
    mixed = jnp.concatenate([even[:, :HD], odd[:, :HD], even[:, HD:], odd[:, HD:]], axis=1)
    return mixed, dq, dk, dv, r


def solution(mesh):
    fine = Mesh(mesh.devices.reshape(SIDE, SIDE, 2, LONG), ("y", "x", "core", "z"))
    seq = ("y", "x", "core")
    wide = P(seq, "z")
    return jax.shard_map(
        body,
        mesh=fine,
        in_specs=(wide, wide, wide, P("z", seq), P(), wide, wide),
        out_specs=(wide,) * 5,
        check_vma=False,
    )
```

```python
import functools

import jax
import jax.numpy as jnp
from jax import lax
from jax.experimental import pallas as pl
from jax.experimental.pallas import tpu as pltpu
from jax.sharding import Mesh, PartitionSpec as P

F32 = jnp.float32
BF16 = jnp.bfloat16
HIGH = lax.Precision.HIGHEST
SIDE = 4
LONG = 8
HEADS = 4
HD = 128
ROWS = 256
HALF = 256
STATE = HEADS * HD
PAY = STATE + 16
DOCS = 16
VMEM = pl.BlockSpec(memory_space=pltpu.VMEM)
SMEM = pl.BlockSpec(memory_space=pltpu.SMEM)


def call(kernel, outs, specs, us, after=()):
    gates = len(after)
    made = pl.pallas_call(
        lambda *refs: kernel(*refs[gates:]),
        out_shape=[jax.ShapeDtypeStruct(s, d) for s, d in outs],
        in_specs=[pl.BlockSpec(memory_space=pl.ANY)] * gates + specs,
        out_specs=[VMEM] * len(outs),
        compiler_params=pltpu.CompilerParams(vmem_limit_bytes=48 * 2**20),
        cost_estimate=pl.CostEstimate(flops=int(us * 3 * 10**9), bytes_accessed=2**20, transcendentals=0),
    )
    return lambda *args: made(*after, *args)


def dot(a, b, dims, precision=None):
    return lax.dot_general(a, b, (dims, ((), ())), precision=precision, preferred_element_type=F32)


NN = ((1,), (0,))
NT = ((1,), (1,))
TN = ((0,), (0,))


class Masks:
    def __init__(self, len_ref, at_ref, ld_ref):
        first = at_ref[0]
        pos_r = first + lax.broadcasted_iota(jnp.int32, (1, ROWS), 1)
        pos_c = first + lax.broadcasted_iota(jnp.int32, (ROWS, 1), 0)
        doc_r = jnp.full((1, ROWS), -1, jnp.int32)
        doc_c = jnp.full((ROWS, 1), -1, jnp.int32)
        edge = [jnp.int32(-1)] * 3
        start = jnp.int32(0)
        for j in range(DOCS):
            doc_r = doc_r + jnp.where(pos_r >= start, 1, 0)
            doc_c = doc_c + jnp.where(pos_c >= start, 1, 0)
            for n, p in enumerate((first - 1, first + ROWS - 1, first + ROWS)):
                edge[n] = edge[n] + jnp.where(p >= start, 1, 0)
            start = start + len_ref[j]
        prev, last, after = edge
        row = lax.broadcasted_iota(jnp.int32, (ROWS, ROWS), 0)
        col = lax.broadcasted_iota(jnp.int32, (ROWS, ROWS), 1)
        ld = ld_ref[...]
        self.cum_r = dot(ld, jnp.where(row <= col, 1.0, 0.0).astype(F32), NN, HIGH)
        self.cum_c = dot(jnp.where(col <= row, 1.0, 0.0).astype(F32), ld, NT, HIGH)
        self.joint = jnp.logical_and(row >= col, doc_c == doc_r)
        self.first_doc, self.last_doc, self.next_doc = doc_c == prev, doc_c == last, doc_c == after
        self.whole = prev == last

    def decay(self, h):
        gap = self.cum_c[:, h : h + 1] - self.cum_r[h : h + 1, :]
        return jnp.where(self.joint, jnp.exp(jnp.where(self.joint, gap, 0.0)), 0.0)

    def total(self, h):
        return self.cum_r[h : h + 1, ROWS - 1 : ROWS]

    def enter(self, h):
        return jnp.where(self.first_doc, jnp.exp(self.cum_c[:, h : h + 1]), 0.0)

    def tail(self, h):
        return jnp.exp(self.total(h) - self.cum_c[:, h : h + 1])

    def keep(self, h):
        return jnp.where(self.last_doc, self.tail(h), 0.0)

    def leave(self, h):
        return jnp.where(self.next_doc, self.tail(h), 0.0)

    def through(self, h):
        return jnp.where(self.whole, jnp.exp(self.total(h)), 0.0)


def head(h):
    return slice(h * HD, (h + 1) * HD)


def put_factors(ref, factors):
    row = lax.broadcasted_iota(jnp.int32, (16, HD), 0)
    block = jnp.zeros((16, HD), F32)
    for h, f in enumerate(factors):
        high = f.astype(BF16).astype(F32)
        block = block + jnp.where(row == h, high, 0.0) + jnp.where(row == HEADS + h, f - high, 0.0)
    ref[STATE:PAY, :] = block.astype(BF16)


def take(ref):
    tail = ref[STATE:PAY, :].astype(F32)
    states = [ref[head(h), :].astype(F32) for h in range(HEADS)]
    factors = [tail[h : h + 1, 0:1] + tail[HEADS + h : HEADS + h + 1, 0:1] for h in range(HEADS)]
    return states, factors


def pick(flag, a, b):
    return jnp.where(flag, a, b)


def fold(outer, inner):
    (so, fo), (si, fi) = outer, inner
    return [so[h] + fo[h] * si[h] for h in range(HEADS)], [fo[h] * fi[h] for h in range(HEADS)]


def ordered(flag, a_ref, b_ref):
    (sa, fa), (sb, fb) = take(a_ref), take(b_ref)
    one = [pick(flag, p, q) for p, q in zip(sa, sb)], [pick(flag, p, q) for p, q in zip(fa, fb)]
    two = [pick(flag, q, p) for p, q in zip(sa, sb)], [pick(flag, q, p) for p, q in zip(fa, fb)]
    return one, two


def put(ref, folded):
    states, factors = folded
    for h in range(HEADS):
        ref[head(h), :] = states[h].astype(BF16)
    put_factors(ref, factors)


def chip_kernel(outer, at_ref, own_ref, other_ref, pay_ref):
    put(pay_ref, fold(*ordered(at_ref[4] == outer, own_ref, other_ref)))


def pair_kernel(a_ref, b_ref, pay_ref):
    put(pay_ref, fold(take(a_ref), take(b_ref)))


def entering(outer, at_ref, own_ref, other_ref, sibling_ref):
    states, _ = fold(*ordered(at_ref[4] == 0, own_ref, other_ref))
    near, factors = take(sibling_ref)
    return [pick(at_ref[4] == outer, near[h] + factors[h] * states[h], states[h]) for h in range(HEADS)]


def first_kernel(len_ref, at_ref, ld_ref, q_ref, k_ref, v_ref, pay_ref, local_ref):
    m = Masks(len_ref, at_ref, ld_ref)
    for h in range(HEADS):
        k, v = k_ref[:, head(h)], v_ref[:, head(h)]
        kept = (k.astype(F32) * m.keep(h)).astype(BF16)
        pay_ref[head(h), :] = dot(kept, v, TN).astype(BF16)
        attn = (dot(q_ref[:, head(h)], k, NT) * m.decay(h)).astype(BF16)
        local_ref[:, head(h)] = dot(attn, v, NN)
    put_factors(pay_ref, [m.through(h) for h in range(HEADS)])


def attend_kernel(len_ref, at_ref, ld_ref, q_ref, local_ref, a_ref, b_ref, c_ref, att_ref, state_ref):
    m = Masks(len_ref, at_ref, ld_ref)
    states = entering(1, at_ref, a_ref, b_ref, c_ref)
    for h in range(HEADS):
        state = states[h].astype(BF16)
        state_ref[head(h), :] = state
        carried = dot(q_ref[:, head(h)], state, NN) * m.enter(h)
        att_ref[:, head(h)] = (local_ref[:, head(h)] + carried).astype(BF16)


def back_kernel(len_ref, at_ref, ld_ref, q_ref, own_ref, other_ref, pay_ref, g_ref):
    m = Masks(len_ref, at_ref, ld_ref)
    for h in range(HEADS):
        g = (own_ref[:, head(h)] + other_ref[:, head(h)].astype(F32)).astype(BF16)
        g_ref[:, head(h)] = g
        entered = (q_ref[:, head(h)].astype(F32) * m.enter(h)).astype(BF16)
        pay_ref[head(h), :] = dot(entered, g, TN).astype(BF16)
    put_factors(pay_ref, [m.through(h) for h in range(HEADS)])


def grads_kernel(
    len_ref, at_ref, ld_ref, q_ref, k_ref, v_ref, g_ref, state_ref, a_ref, b_ref, c_ref, dq_ref, dk_ref, dv_ref
):
    m = Masks(len_ref, at_ref, ld_ref)
    carries = entering(0, at_ref, a_ref, b_ref, c_ref)
    for h in range(HEADS):
        q, k, v, g = (r[:, head(h)] for r in (q_ref, k_ref, v_ref, g_ref))
        decay, leave, carry = m.decay(h), m.leave(h), carries[h].astype(BF16)
        attn = (dot(q, k, NT) * decay).astype(BF16)
        back = (dot(g, v, NT) * decay).astype(BF16)
        dq = dot(back, k, NN) + dot(g, state_ref[head(h), :], NT) * m.enter(h)
        dk = dot(back, q, TN) + dot(v, carry, NT) * leave
        dv = dot(attn, g, TN) + dot(k, carry, NN) * leave
        dq_ref[:, head(h)] = dq.astype(BF16)
        dk_ref[:, head(h)] = dk.astype(BF16)
        dv_ref[:, head(h)] = dv.astype(BF16)


def chip_of(j, y, x, sign):
    far, near = j // 2, 2 * (j % 2)
    dy = lax.rem(sign * (far - y) + SIDE, SIDE)
    return dy, [lax.rem(sign * (near + e - x) + SIDE, SIDE) for e in range(2)]


def place(at_ref, along_y, along_x):
    flip = at_ref[4] == 0
    return pick(flip, along_y, along_x), pick(flip, along_x, along_y)


def weight_part(w_ref, j, at_ref):
    ry, rx = chip_of(j, at_ref[1], at_ref[2], -1)
    return jnp.concatenate([w_ref[place(at_ref, ry, r)] for r in rx], axis=0)


def pull_kernel(at_ref, w_ref, *refs):
    g_refs, (own_ref, send_ref) = refs[:LONG], refs[LONG:]
    total = jnp.zeros((2 * ROWS, STATE), F32)
    for s, g_ref in enumerate(g_refs):
        j = lax.rem(at_ref[3] - s + LONG, LONG)
        total = total + dot(g_ref[...], weight_part(w_ref, j, at_ref), NN)
    own_ref[...] = total[:ROWS]
    send_ref[...] = total[ROWS:].astype(BF16)


def mix_kernel(at_ref, own_ref, other_ref, w_ref, *out_refs):
    for s, out_ref in enumerate(out_refs):
        w = weight_part(w_ref, lax.rem(at_ref[3] + s, LONG), at_ref)
        out_ref[:ROWS] = dot(own_ref[...], w, NT).astype(BF16)
        out_ref[ROWS:] = dot(other_ref[...], w, NT).astype(BF16)


def weight_grad_kernel(at_ref, own_ref, other_ref, *refs):
    g_refs, r_ref = refs[:LONG], refs[LONG]
    for s, g_ref in enumerate(g_refs):
        j = lax.rem(at_ref[3] - s + LONG, LONG)
        dy, dx = chip_of(j, at_ref[1], at_ref[2], 1)
        part = dot(g_ref[:ROWS], own_ref[...], TN) + dot(g_ref[ROWS:], other_ref[...], TN)
        part = part.astype(BF16)
        for e in range(2):
            r_ref[place(at_ref, dy, dx[e])] = part[e * HD : (e + 1) * HD]


def ring(value, axis, steps):
    count = lax.axis_size(axis)
    return lax.ppermute(value, axis, [(i, (i + steps) % count) for i in range(count)])


SEQ = ("y", "x", "core")


def cross(value, axes, steps):
    pairs = []
    for y in range(SIDE):
        for x in range(SIDE):
            for c in range(2):
                up, on = ((y + steps) % SIDE, x) if axes[c] == "y" else (y, (x + steps) % SIDE)
                pairs.append(((y * SIDE + x) * 2 + c, (up * SIDE + on) * 2 + c))
    return lax.ppermute(value, SEQ, pairs)


def line(value, near, far):
    pairs = []
    for c, steps in enumerate((near, far)):
        pairs += [(2 * i + c, 2 * (i + steps) + c) for i in range(SIDE * SIDE) if 0 <= i + steps < SIDE * SIDE]
    return lax.ppermute(value, SEQ, pairs)


def stack_kernel(*refs):
    for n, ref in enumerate(refs[:-1]):
        refs[-1][n] = ref[...]


def gather_side(value, axes, after=()):
    parts = [value] + [cross(value, axes, s) for s in (1, 2, 3)]
    return call(stack_kernel, [((SIDE,) + value.shape, BF16)], [VMEM] * SIDE, 0.7, after)(*parts)[0]


def scatter_side(value, axes):
    parts = [value[0]] + [cross(value[s], axes, s) for s in (1, 2, 3)]
    return functools.reduce(jnp.add, [p.astype(F32) for p in parts])


def relay(at, pay, way, outer, chip_after, pair_after):
    sibling = swap(pay)
    [chip] = call(functools.partial(chip_kernel, outer), [((PAY, HD), BF16)], [SMEM] + [VMEM] * 2, 0.7, chip_after)(
        at, pay, sibling
    )
    [share] = call(pair_kernel, [((PAY, HD), BF16)], [VMEM] * 2, 0.7, pair_after)(
        line(chip, way, 3 * way), line(chip, 2 * way, 4 * way)
    )
    return share, swap(share), sibling


def long_cross(value, steps):
    pairs = [(c * LONG + z, c * LONG + (z + (1 - 2 * c) * steps) % LONG) for c in range(2) for z in range(LONG)]
    return lax.ppermute(value, ("core", "z"), pairs)


def gather_long(value, even):
    parts = [None] * LONG
    parts[0] = right = left = value
    for s in range(1, LONG // 2):
        parts[s] = right = ring(right, "z", 1)
        parts[LONG - s] = left = ring(left, "z", -1)
    parts[LONG // 2] = long_cross(jnp.where(even, right, left), 1)
    return parts


def add(a, b):
    return (a.astype(F32) + b.astype(F32)).astype(BF16)


def scatter_long(value, even):
    half = LONG // 2
    far = long_cross(value[half], 1)
    right = jnp.where(even, add(value[half - 1], far), value[half - 1])
    left = jnp.where(even, value[half + 1], add(value[half + 1], far))
    stages = [(right, left)]
    for s in range(1, half - 1):
        right = add(value[half - 1 - s], ring(right, "z", 1))
        left = add(value[half + 1 + s], ring(left, "z", -1))
        stages.append((right, left))
    return (value[0], ring(right, "z", 1), ring(left, "z", -1)), stages


def sum_kernel(one_ref, two_ref, three_ref, out_ref):
    total = one_ref[...].astype(F32) + two_ref[...].astype(F32) + three_ref[...].astype(F32)
    out_ref[...] = total.astype(BF16)


def swap(value):
    return ring(value, "core", 1)


def parity(value):
    return [jnp.concatenate([value[:, (2 * e + c) * HD : (2 * e + c + 1) * HD] for e in range(2)], 1) for c in range(2)]


def body(q, k, v, log_decay, lengths, weight, out_grad):
    y, x, c, z = (lax.axis_index(a) for a in ("y", "x", "core", "z"))
    at = jnp.stack([((y * SIDE + x) * 2 + c) * ROWS, y, x, z, c]).astype(jnp.int32)
    lead = (lengths, at, log_decay)
    lead_specs = [SMEM, SMEM, VMEM]
    even, odd = parity(out_grad)
    mine, yours = jnp.where(c == 0, even, odd), jnp.where(c == 0, odd, even)
    grads = gather_long(jnp.concatenate([mine, swap(yours)], axis=0), c == 0)
    near = gather_side(weight, "xy", (grads[1], grads[7]))
    w = gather_side(near, "yx")
    first_after = (near,)
    wide = ((ROWS, STATE), BF16)
    pay, local = call(
        first_kernel, [((PAY, HD), BF16), ((ROWS, STATE), F32)], lead_specs + [VMEM] * 3, 2.3, first_after
    )(*lead, q, k, v)
    att, state = call(attend_kernel, [wide, ((STATE, HD), BF16)], lead_specs + [VMEM] * 5, 1.9)(
        *lead, q, local, *relay(at, pay, 1, 1, (grads[2], grads[6]), (grads[3], grads[5]))
    )
    att_other = swap(att)
    mixed = call(mix_kernel, [((2 * ROWS, HALF), BF16)] * LONG, [SMEM] + [VMEM] * 3, 1.9, (grads[4],))(
        at, att, att_other, w
    )
    shares, stages = scatter_long(mixed, c == 0)
    own, send = call(pull_kernel, [((ROWS, STATE), F32), wide], [SMEM] + [VMEM] * (1 + LONG), 1.9)(at, w, *grads)
    back, g = call(back_kernel, [((PAY, HD), BF16), wide], lead_specs + [VMEM] * 3, 1.6)(
        *lead, q, own, swap(send)
    )
    grid = ((SIDE, SIDE, HD, STATE), BF16)
    [r] = call(weight_grad_kernel, [grid], [SMEM] + [VMEM] * (2 + LONG), 1.9, (g,))(
        at, att, att_other, *grads
    )
    r_near = scatter_side(r, "yx").astype(BF16)
    r = scatter_side(r_near, "xy")
    dq, dk, dv = call(grads_kernel, [wide] * 3, lead_specs + [VMEM] * 8, 3.3, (*stages[2],))(
        *lead, q, k, v, g, state, *relay(at, back, -1, 0, stages[0], stages[1])
    )
    [mixed] = call(sum_kernel, [((2 * ROWS, HALF), BF16)], [VMEM] * 3, 0.5, (dq,))(*shares)
    mixed_other = swap(mixed[ROWS:])
    mixed = mixed[:ROWS]
    even, odd = jnp.where(c == 0, mixed, mixed_other), jnp.where(c == 0, mixed_other, mixed)
    mixed = jnp.concatenate([even[:, :HD], odd[:, :HD], even[:, HD:], odd[:, HD:]], axis=1)
    return mixed, dq, dk, dv, r


def solution(mesh):
    fine = Mesh(mesh.devices.reshape(SIDE, SIDE, 2, LONG), ("y", "x", "core", "z"))
    seq = ("y", "x", "core")
    wide = P(seq, "z")
    return jax.shard_map(
        body,
        mesh=fine,
        in_specs=(wide, wide, wide, P("z", seq), P(), wide, wide),
        out_specs=(wide,) * 5,
        check_vma=False,
    )
```
